512 devices in a mesh: expert: 64 (over x, z, core), replica: 8 (over y).
Axes of the slice: x: 4, y: 8, z: 8, core: 2. Of those that a mesh axis runs over, the one named last changes fastest.
Arguments:
- tokens: bfloat16 [65536, 2048], P(('expert', 'replica')), may hold values from -6 to 6
- gate_weight: bfloat16 [64, 2048, 768], P('expert', 'replica'), may hold values from -0.125 to 0.125
- up_weight: bfloat16 [64, 2048, 768], P('expert', 'replica'), may hold values from -0.125 to 0.125
- down_weight: bfloat16 [64, 768, 2048], P('expert', 'replica'), may hold values from -0.21875 to 0.21875
- value_weight: float32 [2048], replicated, may hold values from -1 to 1
- routes: int32 [65536, 1], P(('expert', 'replica')), may hold values from 0 to 63; in each aligned block of 128 rows (0 to 127, 128 to 255, ...) at most 4 rows name the same one
- gates: float32 [65536, 1], P(('expert', 'replica')), may hold values from 0.2 to 1
- node_ids: int32 [512, 128], P(('expert', 'replica')), may hold values from 0 to 15, never falling along the last dimension, each value on 1 to 16 neighbouring positions
- lambda_targets: float32 [512, 16], P(('expert', 'replica')), may hold values from -12 to 12
- above_grad: bfloat16 [65536, 2048], P(('expert', 'replica')), may hold values from -6 to 6
Outputs:
- token_grad: bfloat16 [65536, 2048], P(('expert', 'replica'))
- gate_grad: float32 [65536, 1], P(('expert', 'replica'))
- down_grad: float32 [64, 768, 2048], P('expert', 'replica')
- node_values: float32 [512, 16], P(('expert', 'replica'))
The draws below stay inside these ranges and needn't reach their ends.
Inputs may be any that keep to these rules, and one draw needn't show every extreme that they name: In the rows of one device no expert is named by more than 4 routes, and in every draw some expert is named by exactly 4 routes of some device. `node_ids`: within each row node numbers never fall, and each of the 16 nodes holds 1 to 16 tokens, one of them exactly 16.
All inputs are finite; a program needn't handle non-finite values.
Results may differ from the reference program's by a relative error of at most 0.022.
Values may be sent and summed in bfloat16 or wider, within the bound.
No kernel may reach another device: no remote copies, remote signals or barrier semaphores. Data moves between devices by JAX's collectives and lax.ppermute only.
A program may use at most 64 MiB of HBM per device.

```python
import math
import jax
import jax.numpy as jnp
import numpy as np
from jax import lax

D = 2048
FF = 768
TOP = 1
TOK_DEV = 128
NODE_MOST = 16
EXPERTS = 64
CAP = 4
NODES = 16
GROUPS = 512
TOKENS = 65536
N_EXPERT = 64
N_REPLICA = 8


def steps_of(rng, dims, cuts, smallest, largest):
    factor_of = 1.0
    for position, blocks in cuts:
        heights = jax.random.uniform(jax.random.fold_in(jax.random.fold_in(rng, 6), position), (blocks,), jnp.float32, smallest / len(cuts), largest / len(cuts))
        factor_of = factor_of * jnp.repeat(jnp.exp(heights), dims[position] // blocks).reshape((-1,) + (1,) * (len(dims) - 1 - position))
    return factor_of


def length_profile(number_of, total, limit, skew):
    loads = [(1 << 20) // math.isqrt(grade ** skew) + 1 for grade in range(2, number_of + 1)]
    spare, holding = total - limit - (number_of - 1), [1] * (number_of - 1)
    while spare > 0:
        movable = [i for i in range(number_of - 1) if holding[i] < limit]
        pool, budget = sum([loads[i] for i in movable]), spare
        for i in movable:
            more = min(limit - holding[i], max(1, budget * loads[i] // pool), spare)
            holding[i] = holding[i] + more
            spare = spare - more
    return np.array([limit] + holding)


def ragged_sizes(rng, count, total, most, lean):
    if count == 2:
        one = jax.random.randint(rng, (), max(1, total - most), min(most, total - 1) + 1)
        return jnp.stack([one, total - one])
    lengths = jnp.asarray(length_profile(count, total, most, lean), jnp.int32)
    pairs = (count - 1) // 2
    source_of, taker = lengths[1:1 + 2 * pairs:2], lengths[2:2 + 2 * pairs:2]
    margin = jnp.minimum(source_of - 1, most - taker)
    moved = jax.random.randint(jax.random.fold_in(rng, 1), (pairs,), 0, 1 << 20) % (margin + 1)
    lengths = lengths.at[1:1 + 2 * pairs:2].set(source_of - moved).at[2:2 + 2 * pairs:2].set(taker + moved)
    return lengths[jax.random.permutation(jax.random.fold_in(rng, 2), count)]


def routed_block(stream_key, own, number, rows, count, top, most, skew):
    ranking = jax.random.permutation(stream_key, count)
    heavy_load, common = load_shares(count, rows * top, most, skew, True), load_shares(count, rows * top, most, skew, False)
    places = jnp.arange(count)

    def named(tallies, offset_by):
        used = int((tallies > 0).sum())
        fixed = max(1, used // 4)
        moved = fixed + (places - fixed + offset_by * (used - fixed)) % max(1, count - fixed)
        return jnp.zeros((count,), jnp.int32).at[ranking[jnp.where(places < fixed, places, moved)]].set(jnp.asarray(tallies, jnp.int32))

    tallies = jnp.where(number % 4 == 0, named(heavy_load, number // 4), named(common, number - number // 4 - 1))
    mixed = jax.random.permutation(jax.random.fold_in(own, 3), count)
    giver, sink = mixed[0:count // 2 * 2:2], mixed[1:count // 2 * 2:2]
    room = jnp.minimum(tallies[giver] - 1, most - tallies[sink]) // 2
    room = jnp.where((giver == ranking[0]) | (sink == ranking[0]) | (tallies[sink] == 0), 0, jnp.maximum(room, 0))
    moved = jax.random.randint(jax.random.fold_in(own, 4), (count // 2,), 0, 1 << 20) % (room + 1)
    tallies = tallies.at[giver].add(-moved).at[sink].add(moved)
    items = jnp.searchsorted(jnp.cumsum(tallies), jnp.arange(rows * top), side="right").astype(jnp.int32)
    grid = items.reshape(top, rows).T
    grid = grid[jax.random.permutation(jax.random.fold_in(own, 1), rows)]
    offset_by = jax.random.randint(jax.random.fold_in(own, 2), (rows, 1), 0, top)
    return jnp.take_along_axis(grid, (jnp.arange(top)[None, :] + offset_by) % top, axis=1)


def load_shares(count, total, most, skew, full):
    loads = [(1 << 20) // math.isqrt(grade ** skew) + 1 for grade in range(1, count + 1)]
    largest = most if full else min(most, max(-(-total // count), total * loads[0] // sum(loads)))
    least = 1 if total - largest >= count - 1 else 0
    given, spare = [largest] + [least] * (count - 1), total - largest - least * (count - 1)
    while spare > 0:
        movable = [i for i in range(1, count) if given[i] < largest] or [i for i in range(1, count) if given[i] < most]
        pool, remaining = sum([loads[i] for i in movable]), spare
        for i in movable:
            more = min(most - given[i], max(1, remaining * loads[i] // pool), spare)
            given[i] = given[i] + more
            spare = spare - more
    return np.array(given)


def gaussian(key, extent, width, limit, pieces=(), held_as=jnp.bfloat16):
    result = jax.random.normal(key, extent, jnp.float32) * width
    if len(pieces) > 0:
        result = steps_of(key, extent, pieces, -0.22, 0.18) * result
    return jnp.clip(result, min=-limit, max=limit).astype(held_as)


def setup_inputs(seed: int = 0) -> dict:
    arg_keys = jax.random.split(jax.random.key(seed), 11)
    tokens = gaussian(arg_keys[0], (TOKENS, D), 1.0, 6.0, ((0, 512),))
    gate_weight = gaussian(arg_keys[1], (EXPERTS, D, FF), D ** -0.5, 0.125, ((0, 64), (1, 8)))
    up_weight = gaussian(arg_keys[2], (EXPERTS, D, FF), D ** -0.5, 0.125, ((0, 64), (1, 8)))
    down_weight = gaussian(arg_keys[3], (EXPERTS, FF, D), FF ** -0.5, 0.21875, ((0, 64), (1, 8)))
    value_weight = gaussian(arg_keys[4], (D,), 0.125, 1.0, (), jnp.float32)
    routes_keys = jax.random.split(jax.random.fold_in(arg_keys[5], 1), TOKENS // TOK_DEV)
    routes_turns = jax.random.permutation(jax.random.fold_in(arg_keys[5], 3), TOKENS // TOK_DEV)
    routes = jax.vmap(lambda own, number: routed_block(jax.random.fold_in(arg_keys[5], 2), own, number, TOK_DEV, EXPERTS, TOP, CAP, 2))(routes_keys, routes_turns).reshape((TOKENS, TOP))
    gates = jnp.clip(0.2 + 0.8 * jax.random.uniform(arg_keys[6], (TOKENS, TOP), jnp.float32) ** steps_of(arg_keys[6], (TOKENS, TOP), ((0, 512),), -0.2, 0.2), 0.2, 1.0)
    node_ids = jax.vmap(lambda own: jnp.searchsorted(jnp.cumsum(ragged_sizes(own, NODES, TOK_DEV, NODE_MOST, 1)), jnp.arange(TOK_DEV), side="right"))(jax.random.split(arg_keys[7], GROUPS)).reshape((GROUPS, TOK_DEV)).astype(jnp.int32)
    lambda_targets = gaussian(arg_keys[8], (GROUPS, NODES), 2.0, 12.0, ((0, 512),), jnp.float32)
    above_grad = gaussian(arg_keys[9], (TOKENS, D), 1.0, 6.0, ((0, 512),))
    return dict(tokens=tokens, gate_weight=gate_weight, up_weight=up_weight, down_weight=down_weight, value_weight=value_weight, routes=routes, gates=gates, node_ids=node_ids, lambda_targets=lambda_targets, above_grad=above_grad)


def expert_forward(rows, w_gate, w_up, w_down):
    gate_act = jnp.dot(rows, w_gate, preferred_element_type=jnp.float32)
    up_act = jnp.dot(rows, w_up, preferred_element_type=jnp.float32)
    hidden = (jax.nn.silu(gate_act) * up_act).astype(jnp.bfloat16)
    output = jnp.dot(hidden, w_down, preferred_element_type=jnp.float32).astype(jnp.bfloat16)
    return gate_act, up_act, hidden, output


def reference(tokens, gate_weight, up_weight, down_weight, value_weight, routes, gates, node_ids, lambda_targets, above_grad):
    groups = N_EXPERT * N_REPLICA
    per_group = TOK_DEV * TOP
    total_routes = groups * per_group
    group_routes = routes.reshape(groups, per_group).astype(jnp.int32)
    member = (group_routes[:, :, None] == jnp.arange(EXPERTS, dtype=jnp.int32)[None, None, :]).astype(jnp.int32)
    slot_rank = jnp.sum((jnp.cumsum(member, axis=1) - member) * member, axis=2).astype(jnp.int32)
    group_index = jnp.broadcast_to(jnp.arange(groups, dtype=jnp.int32)[:, None], (groups, per_group))
    route_index = jnp.arange(total_routes, dtype=jnp.int32).reshape(groups, per_group)
    table = jnp.full((EXPERTS, groups, CAP), total_routes, jnp.int32)
    table = table.at[group_routes, group_index, slot_rank].set(route_index)
    table = table.reshape(EXPERTS, groups * CAP)
    flat_table = table.reshape(-1)
    zero_row = jnp.zeros((1, D), jnp.bfloat16)
    token_rows = jnp.concatenate([jnp.repeat(tokens, TOP, axis=0), zero_row], axis=0)
    gate_rows = jnp.concatenate([gates.reshape(total_routes), jnp.zeros((1,), jnp.float32)], axis=0)

    def first_pass(items):
        indices, w_gate, w_up, w_down = items
        output = expert_forward(token_rows[indices], w_gate, w_up, w_down)[3]
        return jnp.sum(output.astype(jnp.float32) * value_weight[None, :], axis=1)

    projected = lax.map(first_pass, (table, gate_weight, up_weight, down_weight))
    route_proj = jnp.zeros((total_routes + 1,), jnp.float32).at[flat_table].set(projected.reshape(-1))[:total_routes]
    token_value = jnp.dot(tokens.astype(jnp.float32), value_weight, precision=lax.Precision.HIGHEST)
    token_value = token_value + jnp.sum((gates.reshape(total_routes) * route_proj).reshape(TOKENS, TOP), axis=1)
    node_member = (node_ids[:, :, None] == jnp.arange(NODES, dtype=jnp.int32)[None, None, :]).astype(jnp.float32)
    counts = jnp.sum(node_member, axis=1)
    node_values = jnp.sum(node_member * token_value.reshape(groups, TOK_DEV)[:, :, None], axis=1) / counts
    token_error = jnp.sum(node_member * (node_values - lambda_targets)[:, None, :], axis=2).reshape(TOKENS)
    value_grad = (above_grad.astype(jnp.float32) + token_error[:, None] * value_weight[None, :]).astype(jnp.bfloat16)
    grad_rows = jnp.concatenate([jnp.repeat(value_grad, TOP, axis=0), zero_row], axis=0)

    def second_pass(items):
        indices, w_gate, w_up, w_down = items
        gate_act, up_act, hidden, output = expert_forward(token_rows[indices], w_gate, w_up, w_down)
        incoming = grad_rows[indices]
        slot_gate_grad = jnp.sum(output.astype(jnp.float32) * incoming.astype(jnp.float32), axis=1)
        out_grad = (gate_rows[indices][:, None] * incoming.astype(jnp.float32)).astype(jnp.bfloat16)
        hidden_grad = jnp.dot(out_grad, w_down.T, preferred_element_type=jnp.float32)
        sig = jax.nn.sigmoid(gate_act)
        silu_val = gate_act * sig
        slope = sig * (1.0 + gate_act * (1.0 - sig))
        gate_back = (hidden_grad * up_act * slope).astype(jnp.bfloat16)
        up_back = (hidden_grad * silu_val).astype(jnp.bfloat16)
        input_grad = (jnp.dot(gate_back, w_gate.T, preferred_element_type=jnp.float32)
                      + jnp.dot(up_back, w_up.T, preferred_element_type=jnp.float32)).astype(jnp.bfloat16)
        hidden_split = hidden.astype(jnp.float32).reshape(N_EXPERT, N_REPLICA, CAP, FF)
        grad_split = out_grad.astype(jnp.float32).reshape(N_EXPERT, N_REPLICA, CAP, D)
        partial_sums = jnp.einsum("irsf,irsd->rfd", hidden_split, grad_split, precision=lax.Precision.HIGHEST)
        rounded = lax.optimization_barrier(partial_sums.astype(jnp.bfloat16))
        weight_grad = jnp.sum(rounded.astype(jnp.float32), axis=0)
        return slot_gate_grad, input_grad, weight_grad

    slot_gates, slot_inputs, down_grad = lax.map(second_pass, (table, gate_weight, up_weight, down_weight))
    route_gate = jnp.zeros((total_routes + 1,), jnp.float32).at[flat_table].set(slot_gates.reshape(-1))[:total_routes]
    route_grad = jnp.zeros((total_routes + 1, D), jnp.float32).at[flat_table].set(slot_inputs.reshape(-1, D).astype(jnp.float32))[:total_routes]
    token_grad = (value_grad.astype(jnp.float32) + jnp.sum(route_grad.reshape(TOKENS, TOP, D), axis=1)).astype(jnp.bfloat16)
    return token_grad, route_gate.reshape(TOKENS, TOP), down_grad, node_values
```

```python
import jax
import jax.numpy as jnp
from jax import lax
from jax.sharding import PartitionSpec as P

BF16 = jnp.bfloat16
F32 = jnp.float32


def exchange(rows):
    return lax.all_to_all(rows, "expert", split_axis=0, concat_axis=0, tiled=True)


def local(
    tokens,
    gate_weight,
    up_weight,
    down_weight,
    value_weight,
    routes,
    gates,
    node_ids,
    lambda_targets,
    above_grad,
):
    experts = lax.axis_size("expert")
    replicas = lax.axis_size("replica")
    tok_rows, width = tokens.shape
    hidden_width = gate_weight.shape[2]
    capacity = 2 * tok_rows // experts
    slots = experts * capacity

    expert_of = routes[:, 0]
    member = (expert_of[:, None] == jnp.arange(experts, dtype=jnp.int32)[None, :]).astype(jnp.int32)
    rank = jnp.sum((jnp.cumsum(member, axis=0) - member) * member, axis=1)
    slot_of = expert_of * capacity + rank
    both_rows = jnp.arange(2 * slots, dtype=jnp.int32)
    both_of = expert_of * (2 * capacity) + rank
    pick = jnp.concatenate([both_of, both_of + capacity])
    pick = (both_rows[:, None] == pick[None, :]).astype(BF16)
    both = jnp.dot(
        pick, jnp.concatenate([tokens, above_grad], axis=0), preferred_element_type=F32
    ).astype(BF16)

    gate_up = lax.all_gather(
        jnp.concatenate([gate_weight[0], up_weight[0]], axis=1), "replica", axis=0, tiled=True
    )
    down = lax.all_gather(down_weight[0], "replica", axis=0, tiled=True)
    head_part = jnp.sum(down_weight[0].astype(F32) * value_weight[None, :], axis=1)
    head = lax.all_to_all(
        jnp.broadcast_to(head_part[None, :], (replicas, hidden_width // replicas)),
        "replica",
        split_axis=0,
        concat_axis=0,
        tiled=True,
    ).reshape(hidden_width)

    both_in = exchange(both.reshape(experts, 2 * capacity, width))
    rows_in = both_in[:, :capacity].reshape(slots, width)
    above_in = both_in[:, capacity:].reshape(slots, width)

    acts = jnp.dot(rows_in, gate_up, preferred_element_type=F32)
    gate_act, up_act = acts[:, :hidden_width], acts[:, hidden_width:]
    sig = jax.nn.sigmoid(gate_act)
    silu = gate_act * sig
    hidden = (silu * up_act).astype(BF16)
    proj = jnp.sum(hidden.astype(F32) * head[None, :], axis=1)
    proj_back = exchange(proj.reshape(experts, capacity)).reshape(slots)

    at_slot = slot_of[:, None] == jnp.arange(slots, dtype=jnp.int32)[None, :]
    route_proj = jnp.sum(jnp.where(at_slot, proj_back[None, :], 0.0), axis=1)
    token_value = jnp.sum(tokens.astype(F32) * value_weight[None, :], axis=1)
    token_value = token_value + gates[:, 0] * route_proj
    nodes = lambda_targets.shape[1]
    in_node = node_ids[0][:, None] == jnp.arange(nodes, dtype=jnp.int32)[None, :]
    in_node = in_node.astype(F32)
    node_mean = jnp.sum(in_node * token_value[:, None], axis=0) / jnp.sum(in_node, axis=0)
    token_error = jnp.sum(in_node * (node_mean - lambda_targets[0])[None, :], axis=1)

    error_slot = jnp.sum(jnp.where(at_slot, token_error[:, None], 0.0), axis=0)
    gate_slot = jnp.sum(jnp.where(at_slot, gates, 0.0), axis=0)
    scalars = jnp.concatenate(
        [error_slot.reshape(experts, capacity), gate_slot.reshape(experts, capacity)], axis=1
    )
    scalars = exchange(scalars)
    error_in = scalars[:, :capacity].reshape(slots)
    gate_in = scalars[:, capacity:].reshape(slots)

    grad_in = (above_in.astype(F32) + error_in[:, None] * value_weight[None, :]).astype(BF16)
    out_grad = (gate_in[:, None] * grad_in.astype(F32)).astype(BF16)
    partial = lax.dot_general(
        hidden, out_grad, (((0,), (0,)), ((), ())), preferred_element_type=F32
    ).astype(BF16)
    down_grad = lax.psum_scatter(partial, "replica", scatter_dimension=0, tiled=True)

    hidden_grad = lax.dot_general(
        out_grad, down, (((1,), (1,)), ((), ())), preferred_element_type=F32
    )
    scaled = jnp.sum(hidden.astype(F32) * hidden_grad, axis=1)
    slope = sig * (1.0 + gate_act * (1.0 - sig))
    back = jnp.concatenate([hidden_grad * up_act * slope, hidden_grad * silu], axis=1).astype(BF16)
    input_grad = lax.dot_general(
        back, gate_up, (((1,), (1,)), ((), ())), preferred_element_type=F32
    ).astype(BF16)
    high = scaled.astype(BF16)
    low = (scaled - high.astype(F32)).astype(BF16)
    lane = jnp.arange(128, dtype=jnp.int32)[None, :]
    tail = jnp.where(lane == 0, high[:, None], jnp.where(lane == 1, low[:, None], 0)).astype(BF16)
    returned = jnp.concatenate([input_grad, tail], axis=1)
    returned = exchange(returned.reshape(experts, capacity, width + 128)).reshape(slots, width + 128)
    route_rows = jnp.dot(at_slot.astype(BF16), returned, preferred_element_type=F32)

    value_grad = (
        above_grad.astype(F32) + token_error[:, None] * value_weight[None, :]
    ).astype(BF16)
    token_grad = (value_grad.astype(F32) + route_rows[:, :width]).astype(BF16)
    gate_grad = (route_rows[:, width : width + 1] + route_rows[:, width + 1 : width + 2]) / gates
    return token_grad, gate_grad, down_grad.astype(F32)[None], node_mean[None, :]


def solution(mesh):
    rows = P(("expert", "replica"), None)
    weight = P("expert", "replica", None)
    return jax.shard_map(
        local,
        mesh=mesh,
        in_specs=(rows, weight, weight, weight, P(), rows, rows, rows, rows, rows),
        out_specs=(rows, rows, weight, rows),
        check_vma=False,
    )
```

```python
import functools

import jax
import jax.numpy as jnp
from jax import lax
from jax.experimental import pallas as pl
from jax.experimental.pallas import tpu as pltpu
from jax.sharding import PartitionSpec as P

BF16 = jnp.bfloat16
F32 = jnp.float32
I32 = jnp.int32
LANES = 128
VMEM = pl.BlockSpec(memory_space=pltpu.VMEM)
SMEM = pl.BlockSpec(memory_space=pltpu.SMEM)
JOIN_FLOPS = 33 * 10**9
EXTRA = 16
NT = (((1,), (1,)), ((), ()))
TN = (((0,), (0,)), ((), ()))


def exchange(rows):
    return lax.all_to_all(rows, "expert", split_axis=0, concat_axis=0, tiled=True)


def shift(block, step):
    count = lax.axis_size("replica")
    return lax.ppermute(block, "replica", [(i, (i + step) % count) for i in range(count)])


def call(body, out_shape, in_specs, flops, moved):
    return pl.pallas_call(
        body,
        out_shape=out_shape,
        in_specs=in_specs,
        out_specs=jax.tree.map(lambda _: VMEM, out_shape),
        cost_estimate=pl.CostEstimate(flops=flops, bytes_accessed=moved, transcendentals=0),
        compiler_params=pltpu.CompilerParams(vmem_limit_bytes=60 * 1024 * 1024),
    )


def iota(shape, axis):
    return lax.broadcasted_iota(I32, shape, axis)


def pack_body(experts, capacity, routes, gates, nodes, tokens, above, out, slot_out):
    rows, width = tokens.shape
    named = routes[...]
    member = (iota((experts, rows), 0) == named).astype(F32)
    before = (iota((rows, rows), 0) < iota((rows, rows), 1)).astype(BF16)
    prior = jnp.dot(member.astype(BF16), before, preferred_element_type=F32)
    rank = jnp.sum(prior * member, axis=0, keepdims=True).astype(I32)
    slot_out[...] = named * capacity + rank
    place = named * (2 * capacity) + rank
    row_of = iota((2 * experts * capacity, rows), 0)
    pick = (row_of == place).astype(BF16)
    pick_above = (row_of == place + capacity).astype(BF16)
    chosen = jnp.dot(pick, tokens[...], preferred_element_type=F32)
    chosen = chosen + jnp.dot(pick_above, above[...], preferred_element_type=F32)
    out[:, :width] = chosen.astype(BF16)
    gate = gates[...]
    high = gate.astype(BF16)
    rest = gate - high.astype(F32)
    middle = rest.astype(BF16)
    low = (rest - middle.astype(F32)).astype(BF16)
    node = nodes[...]
    same = (iota((rows, 16), 1) == node).astype(F32)
    count = jnp.sum(same * jnp.sum(same, axis=0, keepdims=True), axis=1, keepdims=True)
    lane = iota((rows, LANES), 1)
    notes = jnp.where(lane == 0, high.astype(F32), 0.0)
    notes = jnp.where(lane == 1, middle.astype(F32), notes)
    notes = jnp.where(lane == 2, low.astype(F32), notes)
    notes = jnp.where(lane == 3, node.astype(F32), notes)
    notes = jnp.where(lane == 4, count, notes).astype(BF16)
    out[:, width:] = jnp.dot(pick, notes, preferred_element_type=F32).astype(BF16)


def bundle_body(me, gate, down, value_weight, out):
    depth, width = gate.shape
    each = down.shape[0]
    out[:depth, :] = gate[...]
    wanted = value_weight[...]

    def split(value):
        high = value.astype(BF16).astype(F32)
        middle = (value - high).astype(BF16).astype(F32)
        low = (value - high - middle).astype(BF16).astype(F32)
        row = iota((EXTRA, value.shape[1]), 0)
        rows = jnp.where(row == 0, high, jnp.where(row == 1, middle, jnp.where(row == 2, low, 0.0)))
        return rows.astype(BF16)

    three = lax.dot_general(split(wanted), down[...], NT, preferred_element_type=F32)
    head = split(jnp.sum(three, axis=0, keepdims=True))
    place = iota((each, width), 1) == iota((each, width), 0) + me[0] * each
    out[depth:, :] = jnp.dot(head, place.astype(BF16), preferred_element_type=F32).astype(BF16)


def ring_parts(refs, me, count):
    own, far_high, far_low = refs[0], refs[-2], refs[-1]
    rows = own.shape[0]
    parts = [(own, me * rows)]
    for step in range(1, count // 2):
        parts.append((refs[2 * step - 1], lax.rem(me - step + count, count) * rows))
        parts.append((refs[2 * step], lax.rem(me + step, count) * rows))
    far = lax.rem(me + count // 2, count) * rows
    parts.append((far_high, far))
    parts.append((far_low, far + rows // 2))
    return parts


def join_body(count, me, *rest):
    blocks, out = rest[:-1], rest[-1]
    for ref, start in ring_parts(blocks, me[0], count):
        rows = ref.shape[0]
        out[pl.ds(pl.multiple_of(start, 16), rows), :] = ref[...]


def arrive_body(capacity, both, rows, above_out):
    slots, width = above_out.shape
    row = iota((slots, 2 * slots), 0)
    source = row + (row // capacity) * capacity
    column = iota((slots, 2 * slots), 1)
    rows[...] = jnp.dot(
        (column == source).astype(BF16), both[...], preferred_element_type=F32
    ).astype(BF16)
    above = jnp.dot(
        (column == source + capacity).astype(BF16), both[:, :width], preferred_element_type=F32
    )
    above_out[...] = above.astype(BF16)


def forward_body(
    count, capacity, rows, bundles, up, gate_factor, up_factor, hidden_out, note_out, part_out
):
    slots = rows.shape[0]
    width = rows.shape[1] - LANES
    depth = width // count
    gate_act = None
    for owner in range(count):
        part = jnp.dot(
            rows[:, owner * depth : (owner + 1) * depth],
            bundles[owner, :depth, :],
            preferred_element_type=F32,
        )
        gate_act = part if gate_act is None else gate_act + part
    up_act = jnp.dot(rows[:, :width], up[...], preferred_element_type=F32)
    sig = jax.nn.sigmoid(gate_act)
    silu = gate_act * sig
    hidden = (silu * up_act).astype(BF16)
    hidden_out[...] = hidden
    gate_factor[...] = up_act * (sig * (1.0 + gate_act * (1.0 - sig)))
    up_factor[...] = silu
    head = jnp.sum(
        jnp.sum(bundles[:, depth:, :].astype(F32), axis=0), axis=0, keepdims=True
    )
    proj = jnp.sum(hidden.astype(F32) * head, axis=1, keepdims=True)
    notes = rows[:, width:].astype(F32)
    gate = notes[:, 0:1] + notes[:, 1:2] + notes[:, 2:3]
    node = notes[:, 3:4]
    lane = iota((slots, LANES), 1)
    note_out[...] = jnp.where(lane == 0, gate, jnp.where(lane == 1, node, 0.0))
    share = gate * proj / jnp.maximum(notes[:, 4:5], 1.0)
    groups = slots // capacity
    by_node = jnp.where(iota((slots, 16), 1).astype(F32) == node, share, 0.0)
    gather = (iota((groups, slots), 1) // capacity == iota((groups, slots), 0)).astype(F32)
    part_out[...] = jnp.dot(
        gather, by_node, preferred_element_type=F32, precision=lax.Precision.HIGHEST
    )


def partial_body(capacity, sums, notes, above, value_weight, hidden, grad_out, partial_out, error_out):
    slots, width = above.shape
    errors = jnp.sum(sums[...], axis=0, keepdims=True)
    error_out[...] = errors
    lanes = errors.shape[1]
    gate, node = notes[:, 0:1], notes[:, 1:2].astype(I32)
    wanted = (iota((slots, 1), 0) // capacity) * 16 + node
    error = jnp.sum(
        jnp.where(iota((slots, lanes), 1) == wanted, errors, 0.0), axis=1, keepdims=True
    )
    grad = (above[...].astype(F32) + error * value_weight[...]).astype(BF16)
    out_grad = (gate * grad.astype(F32)).astype(BF16)
    grad_out[...] = out_grad
    partial_out[...] = lax.dot_general(
        hidden[...], out_grad, TN, preferred_element_type=F32
    ).astype(BF16)


def backward_body(
    count, grad, down, gate_factor, up_factor, hidden, bundles, up, out, gate_back, up_back
):
    slots, width = grad.shape
    depth = width // count
    hidden_grad = lax.dot_general(grad[...], down[...], NT, preferred_element_type=F32)
    gate_back[...] = (hidden_grad * gate_factor[...]).astype(BF16)
    up_back[...] = (hidden_grad * up_factor[...]).astype(BF16)
    scaled = jnp.sum(hidden[...].astype(F32) * hidden_grad, axis=1, keepdims=True)
    high = scaled.astype(BF16).astype(F32)
    lane = iota((slots, LANES), 1)
    out[:, width:] = jnp.where(
        lane == 0, high, jnp.where(lane == 1, scaled - high, 0.0)
    ).astype(BF16)
    for owner in range(count):
        columns = slice(owner * depth, (owner + 1) * depth)
        part = lax.dot_general(up_back[...], up[columns, :], NT, preferred_element_type=F32)
        part = part + lax.dot_general(
            gate_back[...], bundles[owner, :depth, :], NT, preferred_element_type=F32
        )
        out[:, columns] = part.astype(BF16)


def local(
    tokens,
    gate_weight,
    up_weight,
    down_weight,
    value_weight,
    routes,
    gates,
    node_ids,
    lambda_targets,
    above_grad,
):
    experts = lax.axis_size("expert")
    replicas = lax.axis_size("replica")
    tok_rows, width = tokens.shape
    hidden_width = gate_weight.shape[2]
    capacity = 2 * tok_rows // experts
    slots = experts * capacity
    nodes = lambda_targets.shape[1]
    shape = jax.ShapeDtypeStruct
    value_row = value_weight[None, :]
    me = lax.axis_index("expert")
    my_replica = lax.axis_index("replica").astype(I32).reshape(1)

    bundle = call(
        bundle_body,
        shape((gate_weight.shape[1] + EXTRA, hidden_width), BF16),
        [SMEM, VMEM, VMEM, VMEM],
        0,
        4 * hidden_width * width // replicas,
    )(my_replica, gate_weight[0], down_weight[0], value_row)
    bundles = lax.all_gather(bundle, "replica", axis=0)

    block = up_weight[0]
    blocks = [block]
    right = left = block
    for step in range(1, replicas // 2):
        right, left = shift(right, 1), shift(left, -1)
        blocks += [right, left]
    half = block.shape[0] // 2
    blocks += [shift(right[:half], 1), shift(left[half:], -1)]

    up_full = call(
        functools.partial(join_body, replicas),
        shape((width, hidden_width), BF16),
        [SMEM] + [VMEM] * len(blocks),
        JOIN_FLOPS,
        4 * hidden_width * width,
    )(my_replica, *blocks)

    both, slot_row = call(
        functools.partial(pack_body, experts, capacity),
        [shape((2 * slots, width + LANES), BF16), shape((1, tok_rows), I32)],
        [VMEM] * 5,
        4 * slots * tok_rows * width,
        8 * slots * width,
    )(routes.reshape(1, tok_rows), gates, node_ids.reshape(tok_rows, 1), tokens, above_grad)
    both = exchange(both.reshape(experts, 2 * capacity, width + LANES))
    both = both.reshape(2 * slots, width + LANES)

    rows, above_in = call(
        functools.partial(arrive_body, capacity),
        [shape((slots, width + LANES), BF16), shape((slots, width), BF16)],
        [VMEM],
        4 * slots * slots * width,
        8 * slots * width,
    )(both)
    gate_factor, up_factor, hidden, notes, node_part = call(
        functools.partial(forward_body, replicas, capacity),
        [
            shape((slots, hidden_width), F32),
            shape((slots, hidden_width), F32),
            shape((slots, hidden_width), BF16),
            shape((slots, LANES), F32),
            shape((experts, nodes), F32),
        ],
        [VMEM] * 3,
        4 * slots * hidden_width * width,
        4 * hidden_width * width,
    )(rows, bundles, up_full)
    down = lax.all_gather(down_weight[0], "replica", axis=0, tiled=True)

    in_node = node_ids[0][:, None] == jnp.arange(nodes, dtype=I32)[None, :]
    in_node = in_node.astype(F32)
    token_value = jnp.sum(tokens.astype(F32) * value_row, axis=1)
    own = jnp.sum(in_node * token_value[:, None], axis=0) / jnp.sum(in_node, axis=0)
    own = own - lambda_targets[0]
    is_me = jnp.arange(experts, dtype=I32)[:, None] == me
    node_part = node_part + jnp.where(is_me, own[None, :], 0.0)
    sums = exchange(
        jnp.broadcast_to(node_part.reshape(1, experts * nodes), (experts, experts * nodes))
    )

    out_grad, partial, errors = call(
        functools.partial(partial_body, capacity),
        [
            shape((slots, width), BF16),
            shape((hidden_width, width), BF16),
            shape((1, experts * nodes), F32),
        ],
        [VMEM] * 5,
        2 * slots * hidden_width * width,
        4 * hidden_width * width,
    )(sums, notes, above_in, value_row, hidden)
    down_grad = lax.psum_scatter(partial, "replica", scatter_dimension=0, tiled=True)

    returned, _, _ = call(
        functools.partial(backward_body, replicas),
        [
            shape((slots, width + LANES), BF16),
            shape((slots, hidden_width), BF16),
            shape((slots, hidden_width), BF16),
        ],
        [VMEM] * 7,
        6 * slots * hidden_width * width,
        6 * hidden_width * width,
    )(out_grad, down, gate_factor, up_factor, hidden, bundles, up_full)
    returned = exchange(returned.reshape(experts, capacity, width + LANES))
    returned = returned.reshape(slots, width + LANES)

    node_error = jnp.sum(jnp.where(is_me, errors.reshape(experts, nodes), 0.0), axis=0)
    node_mean = node_error + lambda_targets[0]
    token_error = jnp.sum(in_node * node_error[None, :], axis=1)
    at_slot = slot_row.reshape(tok_rows, 1) == jnp.arange(slots, dtype=I32)[None, :]
    route_rows = jnp.dot(at_slot.astype(BF16), returned, preferred_element_type=F32)
    value_grad = (above_grad.astype(F32) + token_error[:, None] * value_row).astype(BF16)
    token_grad = (value_grad.astype(F32) + route_rows[:, :width]).astype(BF16)
    gate_grad = (route_rows[:, width : width + 1] + route_rows[:, width + 1 : width + 2]) / gates
    return token_grad, gate_grad, down_grad.astype(F32)[None], node_mean[None, :]


def solution(mesh):
    rows = P(("expert", "replica"), None)
    weight = P("expert", "replica", None)
    return jax.shard_map(
        local,
        mesh=mesh,
        in_specs=(rows, weight, weight, weight, P(), rows, rows, rows, rows, rows),
        out_specs=(rows, rows, weight, rows),
        check_vma=False,
    )
```

```python
import functools

import jax
import jax.numpy as jnp
from jax import lax
from jax.experimental import pallas as pl
from jax.experimental.pallas import tpu as pltpu
from jax.sharding import PartitionSpec as P

BF16 = jnp.bfloat16
F32 = jnp.float32
I32 = jnp.int32
LANES = 128
VMEM = pl.BlockSpec(memory_space=pltpu.VMEM)
SMEM = pl.BlockSpec(memory_space=pltpu.SMEM)
JOIN_FLOPS = 33 * 10**9
EXTRA = 16
NT = (((1,), (1,)), ((), ()))
TN = (((0,), (0,)), ((), ()))


def exchange(rows):
    return lax.all_to_all(rows, "expert", split_axis=0, concat_axis=0, tiled=True)


def shift(block, step):
    count = lax.axis_size("replica")
    return lax.ppermute(block, "replica", [(i, (i + step) % count) for i in range(count)])


def call(body, out_shape, in_specs, flops, moved):
    return pl.pallas_call(
        body,
        out_shape=out_shape,
        in_specs=in_specs,
        out_specs=jax.tree.map(lambda _: VMEM, out_shape),
        cost_estimate=pl.CostEstimate(flops=flops, bytes_accessed=moved, transcendentals=0),
        compiler_params=pltpu.CompilerParams(vmem_limit_bytes=60 * 1024 * 1024),
    )


def iota(shape, axis):
    return lax.broadcasted_iota(I32, shape, axis)


def pack_body(experts, capacity, routes, gates, nodes, tokens, above, out, slot_out):
    rows, width = tokens.shape
    named = routes[...]
    member = (iota((experts, rows), 0) == named).astype(F32)
    before = (iota((rows, rows), 0) < iota((rows, rows), 1)).astype(BF16)
    prior = jnp.dot(member.astype(BF16), before, preferred_element_type=F32)
    rank = jnp.sum(prior * member, axis=0, keepdims=True).astype(I32)
    slot_out[...] = named * capacity + rank
    place = named * (2 * capacity) + rank
    row_of = iota((2 * experts * capacity, rows), 0)
    pick = (row_of == place).astype(BF16)
    pick_above = (row_of == place + capacity).astype(BF16)
    chosen = jnp.dot(pick, tokens[...], preferred_element_type=F32)
    chosen = chosen + jnp.dot(pick_above, above[...], preferred_element_type=F32)
    out[:, :width] = chosen.astype(BF16)
    gate = gates[...]
    high = gate.astype(BF16)
    rest = gate - high.astype(F32)
    middle = rest.astype(BF16)
    low = (rest - middle.astype(F32)).astype(BF16)
    node = nodes[...]
    same = (iota((rows, 16), 1) == node).astype(F32)
    count = jnp.sum(same * jnp.sum(same, axis=0, keepdims=True), axis=1, keepdims=True)
    lane = iota((rows, LANES), 1)
    notes = jnp.where(lane == 0, high.astype(F32), 0.0)
    notes = jnp.where(lane == 1, middle.astype(F32), notes)
    notes = jnp.where(lane == 2, low.astype(F32), notes)
    notes = jnp.where(lane == 3, node.astype(F32), notes)
    notes = jnp.where(lane == 4, count, notes).astype(BF16)
    out[:, width:] = jnp.dot(pick, notes, preferred_element_type=F32).astype(BF16)


def bundle_body(me, gate, down, value_weight, out):
    depth, width = gate.shape
    each = down.shape[0]
    out[:depth, :] = gate[...]
    wanted = value_weight[...]

    def split(value):
        high = value.astype(BF16).astype(F32)
        middle = (value - high).astype(BF16).astype(F32)
        low = (value - high - middle).astype(BF16).astype(F32)
        row = iota((EXTRA, value.shape[1]), 0)
        rows = jnp.where(row == 0, high, jnp.where(row == 1, middle, jnp.where(row == 2, low, 0.0)))
        return rows.astype(BF16)

    three = lax.dot_general(split(wanted), down[...], NT, preferred_element_type=F32)
    head = split(jnp.sum(three, axis=0, keepdims=True))
    place = iota((each, width), 1) == iota((each, width), 0) + me[0] * each
    out[depth:, :] = jnp.dot(head, place.astype(BF16), preferred_element_type=F32).astype(BF16)


def ring_owners(me, count):
    owners = [me]
    for step in range(1, count // 2):
        owners.append(lax.rem(me - step + count, count))
        owners.append(lax.rem(me + step, count))
    return owners + [lax.rem(me + count // 2, count)]


def join_body(high, low, out):
    rows = high.shape[0]
    out[:rows, :] = high[...]
    out[rows:, :] = low[...]


def forward_body(count, capacity, me, both, bundles, *rest):
    blocks, rest = rest[:count], rest[count:]
    above_out, gate_factor, up_factor, hidden_out, note_out, part_out, rows = rest
    slots, width = above_out.shape
    depth = width // count
    row = iota((slots, 2 * slots), 0)
    source = row + (row // capacity) * capacity
    column = iota((slots, 2 * slots), 1)
    rows[...] = jnp.dot(
        (column == source).astype(BF16), both[...], preferred_element_type=F32
    ).astype(BF16)
    above = jnp.dot(
        (column == source + capacity).astype(BF16), both[:, :width], preferred_element_type=F32
    )
    above_out[...] = above.astype(BF16)
    up_act = None
    for owner, ref in zip(ring_owners(me[0], count), blocks, strict=True):
        columns = pl.ds(pl.multiple_of(owner * depth, 128), depth)
        part = jnp.dot(rows[:, columns], ref[...], preferred_element_type=F32)
        up_act = part if up_act is None else up_act + part
    gate_act = None
    for owner in range(count):
        part = jnp.dot(
            rows[:, owner * depth : (owner + 1) * depth],
            bundles[owner, :depth, :],
            preferred_element_type=F32,
        )
        gate_act = part if gate_act is None else gate_act + part
    sig = jax.nn.sigmoid(gate_act)
    silu = gate_act * sig
    hidden = (silu * up_act).astype(BF16)
    hidden_out[...] = hidden
    gate_factor[...] = (up_act * (sig * (1.0 + gate_act * (1.0 - sig)))).astype(BF16)
    up_factor[...] = silu.astype(BF16)
    head = jnp.sum(
        jnp.sum(bundles[:, depth:, :].astype(F32), axis=0), axis=0, keepdims=True
    )
    proj = jnp.sum(hidden.astype(F32) * head, axis=1, keepdims=True)
    notes = rows[:, width:].astype(F32)
    gate = notes[:, 0:1] + notes[:, 1:2] + notes[:, 2:3]
    node = notes[:, 3:4]
    lane = iota((slots, LANES), 1)
    note_out[...] = jnp.where(lane == 0, gate, jnp.where(lane == 1, node, 0.0))
    share = gate * proj / jnp.maximum(notes[:, 4:5], 1.0)
    groups = slots // capacity
    by_node = jnp.where(iota((slots, 16), 1).astype(F32) == node, share, 0.0)
    gather = (iota((groups, slots), 1) // capacity == iota((groups, slots), 0)).astype(F32)
    part_out[...] = jnp.dot(
        gather, by_node, preferred_element_type=F32, precision=lax.Precision.HIGHEST
    )


def partial_body(capacity, sums, notes, above, value_weight, hidden, grad_out, partial_out, error_out):
    slots, width = above.shape
    errors = jnp.sum(sums[...], axis=0, keepdims=True)
    error_out[...] = errors
    lanes = errors.shape[1]
    gate, node = notes[:, 0:1], notes[:, 1:2].astype(I32)
    wanted = (iota((slots, 1), 0) // capacity) * 16 + node
    error = jnp.sum(
        jnp.where(iota((slots, lanes), 1) == wanted, errors, 0.0), axis=1, keepdims=True
    )
    grad = (above[...].astype(F32) + error * value_weight[...]).astype(BF16)
    out_grad = (gate * grad.astype(F32)).astype(BF16)
    grad_out[...] = out_grad
    partial_out[...] = lax.dot_general(
        hidden[...], out_grad, TN, preferred_element_type=F32
    ).astype(BF16)


def backward_body(count, me, grad, down, gate_factor, up_factor, hidden, bundles, *rest):
    blocks, (out, gate_back, up_back) = rest[:count], rest[count:]
    slots, width = grad.shape
    depth = width // count
    hidden_grad = lax.dot_general(grad[...], down[...], NT, preferred_element_type=F32)
    gate_back[...] = (hidden_grad * gate_factor[...].astype(F32)).astype(BF16)
    up_back[...] = (hidden_grad * up_factor[...].astype(F32)).astype(BF16)
    scaled = jnp.sum(hidden[...].astype(F32) * hidden_grad, axis=1, keepdims=True)
    high = scaled.astype(BF16).astype(F32)
    lane = iota((slots, LANES), 1)
    out[:, width:] = jnp.where(
        lane == 0, high, jnp.where(lane == 1, scaled - high, 0.0)
    ).astype(BF16)
    for owner, ref in zip(ring_owners(me[0], count), blocks, strict=True):
        part = lax.dot_general(up_back[...], ref[...], NT, preferred_element_type=F32)
        part = part + lax.dot_general(
            gate_back[...], bundles[owner, :depth, :], NT, preferred_element_type=F32
        )
        out[:, pl.ds(pl.multiple_of(owner * depth, 128), depth)] = part.astype(BF16)


def finish_body(returned, slot, above, value_weight, error, gates, sums, token_out, gate_out, down_out):
    slots = returned.shape[0]
    rows, width = above.shape
    pick = (iota((slots, rows), 0) == slot[...]).astype(BF16)
    mine = lax.dot_general(pick, returned[...], TN, preferred_element_type=F32)
    grad = (above[...].astype(F32) + error[...] * value_weight[...]).astype(BF16)
    token_out[...] = (grad.astype(F32) + mine[:, :width]).astype(BF16)
    gate_out[...] = (mine[:, width : width + 1] + mine[:, width + 1 : width + 2]) / gates[...]
    down_out[...] = sums[...].astype(F32)


def local(
    tokens,
    gate_weight,
    up_weight,
    down_weight,
    value_weight,
    routes,
    gates,
    node_ids,
    lambda_targets,
    above_grad,
):
    experts = lax.axis_size("expert")
    replicas = lax.axis_size("replica")
    tok_rows, width = tokens.shape
    hidden_width = gate_weight.shape[2]
    capacity = 2 * tok_rows // experts
    slots = experts * capacity
    nodes = lambda_targets.shape[1]
    shape = jax.ShapeDtypeStruct
    value_row = value_weight[None, :]
    me = lax.axis_index("expert")
    my_replica = lax.axis_index("replica").astype(I32).reshape(1)

    bundle = call(
        bundle_body,
        shape((gate_weight.shape[1] + EXTRA, hidden_width), BF16),
        [SMEM, VMEM, VMEM, VMEM],
        0,
        4 * hidden_width * width // replicas,
    )(my_replica, gate_weight[0], down_weight[0], value_row)
    bundles = lax.all_gather(bundle, "replica", axis=0)

    block = up_weight[0]
    blocks = [block]
    right = left = block
    for step in range(1, replicas // 2):
        right, left = shift(right, 1), shift(left, -1)
        blocks += [right, left]
    half = block.shape[0] // 2
    blocks += [shift(right[:half], 1), shift(left[half:], -1)]

    blocks[-2:] = [
        call(join_body, shape(block.shape, BF16), [VMEM] * 2, JOIN_FLOPS, 4 * half * hidden_width)(
            *blocks[-2:]
        )
    ]

    both, slot_row = call(
        functools.partial(pack_body, experts, capacity),
        [shape((2 * slots, width + LANES), BF16), shape((1, tok_rows), I32)],
        [VMEM] * 5,
        4 * slots * tok_rows * width,
        8 * slots * width,
    )(routes.reshape(1, tok_rows), gates, node_ids.reshape(tok_rows, 1), tokens, above_grad)
    both = exchange(both.reshape(experts, 2 * capacity, width + LANES))
    both = both.reshape(2 * slots, width + LANES)

    above_in, gate_factor, up_factor, hidden, notes, node_part, _ = call(
        functools.partial(forward_body, replicas, capacity),
        [
            shape((slots, width), BF16),
            shape((slots, hidden_width), BF16),
            shape((slots, hidden_width), BF16),
            shape((slots, hidden_width), BF16),
            shape((slots, LANES), F32),
            shape((experts, nodes), F32),
            shape((slots, width + LANES), BF16),
        ],
        [SMEM] + [VMEM] * (2 + replicas),
        4 * slots * hidden_width * width,
        4 * hidden_width * width,
    )(my_replica, both, bundles, *blocks)
    down = lax.all_gather(down_weight[0], "replica", axis=0, tiled=True)

    in_node = node_ids[0][:, None] == jnp.arange(nodes, dtype=I32)[None, :]
    in_node = in_node.astype(F32)
    token_value = jnp.sum(tokens.astype(F32) * value_row, axis=1)
    own = jnp.sum(in_node * token_value[:, None], axis=0) / jnp.sum(in_node, axis=0)
    own = own - lambda_targets[0]
    is_me = jnp.arange(experts, dtype=I32)[:, None] == me
    node_part = node_part + jnp.where(is_me, own[None, :], 0.0)
    sums = exchange(
        jnp.broadcast_to(node_part.reshape(1, experts * nodes), (experts, experts * nodes))
    )

    out_grad, partial, errors = call(
        functools.partial(partial_body, capacity),
        [
            shape((slots, width), BF16),
            shape((hidden_width, width), BF16),
            shape((1, experts * nodes), F32),
        ],
        [VMEM] * 5,
        2 * slots * hidden_width * width,
        4 * hidden_width * width,
    )(sums, notes, above_in, value_row, hidden)
    down_grad = lax.psum_scatter(partial, "replica", scatter_dimension=0, tiled=True)

    returned, _, _ = call(
        functools.partial(backward_body, replicas),
        [
            shape((slots, width + LANES), BF16),
            shape((slots, hidden_width), BF16),
            shape((slots, hidden_width), BF16),
        ],
        [SMEM] + [VMEM] * (6 + replicas),
        6 * slots * hidden_width * width,
        6 * hidden_width * width,
    )(my_replica, out_grad, down, gate_factor, up_factor, hidden, bundles, *blocks)
    returned = exchange(returned.reshape(experts, capacity, width + LANES))
    returned = returned.reshape(slots, width + LANES)

    node_error = jnp.sum(jnp.where(is_me, errors.reshape(experts, nodes), 0.0), axis=0)
    node_mean = node_error + lambda_targets[0]
    token_error = jnp.sum(in_node * node_error[None, :], axis=1)
    token_grad, gate_grad, down_out = call(
        finish_body,
        [
            shape(tokens.shape, BF16),
            shape(gates.shape, F32),
            shape(down_grad.shape, F32),
        ],
        [VMEM] * 7,
        2 * slots * tok_rows * width,
        8 * slots * width,
    )(returned, slot_row, above_grad, value_row, token_error[:, None], gates, down_grad)
    return token_grad, gate_grad, down_out[None], node_mean[None, :]


def solution(mesh):
    rows = P(("expert", "replica"), None)
    weight = P("expert", "replica", None)
    return jax.shard_map(
        local,
        mesh=mesh,
        in_specs=(rows, weight, weight, weight, P(), rows, rows, rows, rows, rows),
        out_specs=(rows, rows, weight, rows),
        check_vma=False,
    )
```

```python
import functools

import jax
import jax.numpy as jnp
from jax import lax
from jax.experimental import pallas as pl
from jax.experimental.pallas import tpu as pltpu
from jax.sharding import PartitionSpec as P

BF16 = jnp.bfloat16
F32 = jnp.float32
I32 = jnp.int32
LANES = 128
VMEM = pl.BlockSpec(memory_space=pltpu.VMEM)
SMEM = pl.BlockSpec(memory_space=pltpu.SMEM)
JOIN_FLOPS = 33 * 10**9
EXTRA = 16
NT = (((1,), (1,)), ((), ()))
TN = (((0,), (0,)), ((), ()))


def exchange(rows):
    return lax.all_to_all(rows, "expert", split_axis=0, concat_axis=0, tiled=True)


def shift(block, step):
    count = lax.axis_size("replica")
    return lax.ppermute(block, "replica", [(i, (i + step) % count) for i in range(count)])


def call(body, out_shape, in_specs, flops, moved):
    return pl.pallas_call(
        body,
        out_shape=out_shape,
        in_specs=in_specs,
        out_specs=jax.tree.map(lambda _: VMEM, out_shape),
        cost_estimate=pl.CostEstimate(flops=flops, bytes_accessed=moved, transcendentals=0),
        compiler_params=pltpu.CompilerParams(vmem_limit_bytes=60 * 1024 * 1024),
    )


def iota(shape, axis):
    return lax.broadcasted_iota(I32, shape, axis)


def pack_body(experts, capacity, routes, gates, nodes, tokens, above, out, slot_out):
    rows, width = tokens.shape
    named = routes[...]
    member = (iota((experts, rows), 0) == named).astype(F32)
    before = (iota((rows, rows), 0) < iota((rows, rows), 1)).astype(BF16)
    prior = jnp.dot(member.astype(BF16), before, preferred_element_type=F32)
    rank = jnp.sum(prior * member, axis=0, keepdims=True).astype(I32)
    slot_out[...] = named * capacity + rank
    place = named * (2 * capacity) + rank
    row_of = iota((2 * experts * capacity, rows), 0)
    pick = (row_of == place).astype(BF16)
    pick_above = (row_of == place + capacity).astype(BF16)
    chosen = jnp.dot(pick, tokens[...], preferred_element_type=F32)
    chosen = chosen + jnp.dot(pick_above, above[...], preferred_element_type=F32)
    out[:, :width] = chosen.astype(BF16)
    gate = gates[...]
    high = gate.astype(BF16).astype(F32)
    middle = (gate - high).astype(BF16).astype(F32)
    low = gate - high - middle
    node = nodes[...]
    same = (iota((16, rows), 0) == node).astype(F32)
    count = jnp.sum(same * jnp.sum(same, axis=1, keepdims=True), axis=0, keepdims=True)
    lane = iota((LANES, rows), 0)
    notes = jnp.where(lane == 0, high, jnp.where(lane == 1, middle, jnp.where(lane == 2, low, 0.0)))
    notes = jnp.where(lane == 3, node.astype(F32), jnp.where(lane == 4, count, notes))
    out[:, width:] = lax.dot_general(
        pick, notes.astype(BF16), NT, preferred_element_type=F32
    ).astype(BF16)


def bundle_body(me, gate, down, value_weight, out):
    depth, width = gate.shape
    each = down.shape[0]
    out[:depth, :] = gate[...]
    wanted = value_weight[...]

    def split(value):
        high = value.astype(BF16).astype(F32)
        middle = (value - high).astype(BF16).astype(F32)
        low = (value - high - middle).astype(BF16).astype(F32)
        row = iota((EXTRA, value.shape[1]), 0)
        rows = jnp.where(row == 0, high, jnp.where(row == 1, middle, jnp.where(row == 2, low, 0.0)))
        return rows.astype(BF16)

    three = lax.dot_general(split(wanted), down[...], NT, preferred_element_type=F32)
    head = split(jnp.sum(three, axis=0, keepdims=True))
    place = iota((each, width), 1) == iota((each, width), 0) + me[0] * each
    out[depth:, :] = jnp.dot(head, place.astype(BF16), preferred_element_type=F32).astype(BF16)


def ring_owners(me, count):
    owners = [me]
    for step in range(1, count // 2):
        owners.append(lax.rem(me - step + count, count))
        owners.append(lax.rem(me + step, count))
    return owners + [lax.rem(me + count // 2, count)]


def join_body(high, low, out):
    rows = high.shape[0]
    out[:rows, :] = high[...]
    out[rows:, :] = low[...]


def forward_body(count, capacity, me, both, bundles, *rest):
    blocks, rest = rest[:count], rest[count:]
    above_out, gate_factor, up_factor, hidden_out, note_out, part_out, rows = rest
    slots, width = above_out.shape
    depth = width // count
    row = iota((slots, 2 * slots), 0)
    source = row + (row // capacity) * capacity
    column = iota((slots, 2 * slots), 1)
    rows[...] = jnp.dot(
        (column == source).astype(BF16), both[...], preferred_element_type=F32
    ).astype(BF16)
    above = jnp.dot(
        (column == source + capacity).astype(BF16), both[:, :width], preferred_element_type=F32
    )
    above_out[...] = above.astype(BF16)
    up_act = None
    for owner, ref in zip(ring_owners(me[0], count), blocks, strict=True):
        columns = pl.ds(pl.multiple_of(owner * depth, 128), depth)
        part = jnp.dot(rows[:, columns], ref[...], preferred_element_type=F32)
        up_act = part if up_act is None else up_act + part
    gate_act = None
    for owner in range(count):
        part = jnp.dot(
            rows[:, owner * depth : (owner + 1) * depth],
            bundles[owner, :depth, :],
            preferred_element_type=F32,
        )
        gate_act = part if gate_act is None else gate_act + part
    sig = jax.nn.sigmoid(gate_act)
    silu = gate_act * sig
    hidden = (silu * up_act).astype(BF16)
    hidden_out[...] = hidden
    gate_factor[...] = (up_act * (sig * (1.0 + gate_act * (1.0 - sig)))).astype(BF16)
    up_factor[...] = silu.astype(BF16)
    head = jnp.sum(
        jnp.sum(bundles[:, depth:, :].astype(F32), axis=0), axis=0, keepdims=True
    )
    proj = jnp.sum(hidden.astype(F32) * head, axis=1, keepdims=True)
    notes = rows[:, width:].astype(F32)
    gate = notes[:, 0:1] + notes[:, 1:2] + notes[:, 2:3]
    node = notes[:, 3:4]
    lane = iota((slots, LANES), 1)
    note_out[...] = jnp.where(lane == 0, gate, jnp.where(lane == 1, node, 0.0))
    share = gate * proj / jnp.maximum(notes[:, 4:5], 1.0)
    groups = slots // capacity
    by_node = jnp.where(iota((slots, 16), 1).astype(F32) == node, share, 0.0)
    gather = (iota((groups, slots), 1) // capacity == iota((groups, slots), 0)).astype(F32)
    part_out[...] = jnp.dot(
        gather, by_node, preferred_element_type=F32, precision=lax.Precision.HIGHEST
    )


def partial_body(capacity, sums, notes, above, value_weight, hidden, grad_out, partial_out, error_out):
    slots, width = above.shape
    errors = jnp.sum(sums[...], axis=0, keepdims=True)
    error_out[...] = errors
    lanes = errors.shape[1]
    gate, node = notes[:, 0:1], notes[:, 1:2].astype(I32)
    wanted = (iota((slots, 1), 0) // capacity) * 16 + node
    error = jnp.sum(
        jnp.where(iota((slots, lanes), 1) == wanted, errors, 0.0), axis=1, keepdims=True
    )
    grad = (above[...].astype(F32) + error * value_weight[...]).astype(BF16)
    out_grad = (gate * grad.astype(F32)).astype(BF16)
    grad_out[...] = out_grad
    partial_out[...] = lax.dot_general(
        hidden[...], out_grad, TN, preferred_element_type=F32
    ).astype(BF16)


def backward_body(count, me, grad, down, gate_factor, up_factor, hidden, bundles, *rest):
    blocks, (out, gate_back, up_back) = rest[:count], rest[count:]
    slots, width = grad.shape
    depth = width // count
    hidden_grad = lax.dot_general(grad[...], down[...], NT, preferred_element_type=F32)
    gate_back[...] = (hidden_grad * gate_factor[...].astype(F32)).astype(BF16)
    up_back[...] = (hidden_grad * up_factor[...].astype(F32)).astype(BF16)
    scaled = jnp.sum(hidden[...].astype(F32) * hidden_grad, axis=1, keepdims=True)
    high = scaled.astype(BF16).astype(F32)
    lane = iota((slots, LANES), 1)
    out[:, width:] = jnp.where(
        lane == 0, high, jnp.where(lane == 1, scaled - high, 0.0)
    ).astype(BF16)
    for owner, ref in zip(ring_owners(me[0], count), blocks, strict=True):
        part = lax.dot_general(up_back[...], ref[...], NT, preferred_element_type=F32)
        part = part + lax.dot_general(
            gate_back[...], bundles[owner, :depth, :], NT, preferred_element_type=F32
        )
        out[:, pl.ds(pl.multiple_of(owner * depth, 128), depth)] = part.astype(BF16)


def finish_body(returned, slot, above, value_weight, error, gates, sums, token_out, gate_out, down_out):
    slots = returned.shape[0]
    rows, width = above.shape
    pick = (iota((slots, rows), 0) == slot[...]).astype(BF16)
    mine = lax.dot_general(pick, returned[:, :width], TN, preferred_element_type=F32)
    grad = (above[...].astype(F32) + error[...] * value_weight[...]).astype(BF16)
    token_out[...] = (grad.astype(F32) + mine).astype(BF16)
    tail = lax.dot_general(returned[:, width:], pick, TN, preferred_element_type=F32)
    gate_out[...] = (tail[0:1, :] + tail[1:2, :]) / gates[...]
    down_out[...] = sums[...].astype(F32)


def local(
    tokens,
    gate_weight,
    up_weight,
    down_weight,
    value_weight,
    routes,
    gates,
    node_ids,
    lambda_targets,
    above_grad,
):
    experts = lax.axis_size("expert")
    replicas = lax.axis_size("replica")
    tok_rows, width = tokens.shape
    hidden_width = gate_weight.shape[2]
    capacity = 2 * tok_rows // experts
    slots = experts * capacity
    nodes = lambda_targets.shape[1]
    shape = jax.ShapeDtypeStruct
    value_row = value_weight[None, :]
    gate_row = gates.reshape(1, tok_rows)
    me = lax.axis_index("expert")
    my_replica = lax.axis_index("replica").astype(I32).reshape(1)

    bundle = call(
        bundle_body,
        shape((gate_weight.shape[1] + EXTRA, hidden_width), BF16),
        [SMEM, VMEM, VMEM, VMEM],
        0,
        4 * hidden_width * width // replicas,
    )(my_replica, gate_weight[0], down_weight[0], value_row)
    bundles = lax.all_gather(bundle, "replica", axis=0)

    block = up_weight[0]
    blocks = [block]
    right = left = block
    for step in range(1, replicas // 2):
        right, left = shift(right, 1), shift(left, -1)
        blocks += [right, left]
    half = block.shape[0] // 2
    blocks += [shift(right[:half], 1), shift(left[half:], -1)]

    blocks[-2:] = [
        call(join_body, shape(block.shape, BF16), [VMEM] * 2, JOIN_FLOPS, 4 * half * hidden_width)(
            *blocks[-2:]
        )
    ]

    both, slot_row = call(
        functools.partial(pack_body, experts, capacity),
        [shape((2 * slots, width + LANES), BF16), shape((1, tok_rows), I32)],
        [VMEM] * 5,
        4 * slots * tok_rows * width,
        8 * slots * width,
    )(routes.reshape(1, tok_rows), gate_row, node_ids, tokens, above_grad)
    both = exchange(both.reshape(experts, 2 * capacity, width + LANES))
    both = both.reshape(2 * slots, width + LANES)

    above_in, gate_factor, up_factor, hidden, notes, node_part, _ = call(
        functools.partial(forward_body, replicas, capacity),
        [
            shape((slots, width), BF16),
            shape((slots, hidden_width), BF16),
            shape((slots, hidden_width), BF16),
            shape((slots, hidden_width), BF16),
            shape((slots, LANES), F32),
            shape((experts, nodes), F32),
            shape((slots, width + LANES), BF16),
        ],
        [SMEM] + [VMEM] * (2 + replicas),
        4 * slots * hidden_width * width,
        4 * hidden_width * width,
    )(my_replica, both, bundles, *blocks)
    down = lax.all_gather(down_weight[0], "replica", axis=0, tiled=True)

    in_node = node_ids[0][:, None] == jnp.arange(nodes, dtype=I32)[None, :]
    in_node = in_node.astype(F32)
    token_value = jnp.sum(tokens.astype(F32) * value_row, axis=1)
    own = jnp.sum(in_node * token_value[:, None], axis=0) / jnp.sum(in_node, axis=0)
    own = own - lambda_targets[0]
    is_me = jnp.arange(experts, dtype=I32)[:, None] == me
    node_part = node_part + jnp.where(is_me, own[None, :], 0.0)
    sums = exchange(
        jnp.broadcast_to(node_part.reshape(1, experts * nodes), (experts, experts * nodes))
    )

    out_grad, partial, errors = call(
        functools.partial(partial_body, capacity),
        [
            shape((slots, width), BF16),
            shape((hidden_width, width), BF16),
            shape((1, experts * nodes), F32),
        ],
        [VMEM] * 5,
        2 * slots * hidden_width * width,
        4 * hidden_width * width,
    )(sums, notes, above_in, value_row, hidden)
    down_grad = lax.psum_scatter(partial, "replica", scatter_dimension=0, tiled=True)

    returned, _, _ = call(
        functools.partial(backward_body, replicas),
        [
            shape((slots, width + LANES), BF16),
            shape((slots, hidden_width), BF16),
            shape((slots, hidden_width), BF16),
        ],
        [SMEM] + [VMEM] * (6 + replicas),
        6 * slots * hidden_width * width,
        6 * hidden_width * width,
    )(my_replica, out_grad, down, gate_factor, up_factor, hidden, bundles, *blocks)
    returned = exchange(returned.reshape(experts, capacity, width + LANES))
    returned = returned.reshape(slots, width + LANES)

    node_error = jnp.sum(jnp.where(is_me, errors.reshape(experts, nodes), 0.0), axis=0)
    node_mean = node_error + lambda_targets[0]
    token_error = jnp.sum(in_node * node_error[None, :], axis=1)
    token_grad, gate_grad, down_out = call(
        finish_body,
        [
            shape(tokens.shape, BF16),
            shape(gate_row.shape, F32),
            shape(down_grad.shape, F32),
        ],
        [VMEM] * 7,
        2 * slots * tok_rows * width,
        8 * slots * width,
    )(returned, slot_row, above_grad, value_row, token_error[:, None], gate_row, down_grad)
    return token_grad, gate_grad.reshape(gates.shape), down_out[None], node_mean[None, :]


def solution(mesh):
    rows = P(("expert", "replica"), None)
    weight = P("expert", "replica", None)
    return jax.shard_map(
        local,
        mesh=mesh,
        in_specs=(rows, weight, weight, weight, P(), rows, rows, rows, rows, rows),
        out_specs=(rows, rows, weight, rows),
        check_vma=False,
    )
```

```python
import functools

import jax
import jax.numpy as jnp
from jax import lax
from jax.experimental import pallas as pl
from jax.experimental.pallas import tpu as pltpu
from jax.sharding import PartitionSpec as P

BF16 = jnp.bfloat16
F32 = jnp.float32
I32 = jnp.int32
LANES = 128
VMEM = pl.BlockSpec(memory_space=pltpu.VMEM)
SMEM = pl.BlockSpec(memory_space=pltpu.SMEM)
JOIN_FLOPS = 33 * 10**9
EXTRA = 16
NT = (((1,), (1,)), ((), ()))
TN = (((0,), (0,)), ((), ()))


def exchange(rows):
    return lax.all_to_all(rows, "expert", split_axis=0, concat_axis=0, tiled=True)


def shift(block, step):
    count = lax.axis_size("replica")
    return lax.ppermute(block, "replica", [(i, (i + step) % count) for i in range(count)])


def call(body, out_shape, in_specs, flops, moved):
    return pl.pallas_call(
        body,
        out_shape=out_shape,
        in_specs=in_specs,
        out_specs=jax.tree.map(lambda _: VMEM, out_shape),
        cost_estimate=pl.CostEstimate(flops=flops, bytes_accessed=moved, transcendentals=0),
        compiler_params=pltpu.CompilerParams(vmem_limit_bytes=32 * 1024 * 1024),
    )


def iota(shape, axis):
    return lax.broadcasted_iota(I32, shape, axis)


def pack_body(experts, capacity, routes, gates, nodes, tokens, above, out, slot_out):
    rows, width = tokens.shape
    named = routes[...]
    member = (iota((experts, rows), 0) == named).astype(F32)
    before = (iota((rows, rows), 0) < iota((rows, rows), 1)).astype(BF16)
    prior = jnp.dot(member.astype(BF16), before, preferred_element_type=F32)
    rank = jnp.sum(prior * member, axis=0, keepdims=True).astype(I32)
    slot_out[...] = named * capacity + rank
    place = named * (2 * capacity) + rank
    row_of = iota((2 * experts * capacity, rows), 0)
    pick = (row_of == place).astype(BF16)
    pick_above = (row_of == place + capacity).astype(BF16)
    chosen = jnp.dot(pick, tokens[...], preferred_element_type=F32)
    chosen = chosen + jnp.dot(pick_above, above[...], preferred_element_type=F32)
    out[:, :width] = chosen.astype(BF16)
    gate = gates[...]
    high = gate.astype(BF16).astype(F32)
    middle = (gate - high).astype(BF16).astype(F32)
    low = gate - high - middle
    node = nodes[...]
    same = (iota((16, rows), 0) == node).astype(F32)
    count = jnp.sum(same * jnp.sum(same, axis=1, keepdims=True), axis=0, keepdims=True)
    lane = iota((LANES, rows), 0)
    notes = jnp.where(lane == 0, high, jnp.where(lane == 1, middle, jnp.where(lane == 2, low, 0.0)))
    notes = jnp.where(lane == 3, node.astype(F32), jnp.where(lane == 4, count, notes))
    out[:, width:] = lax.dot_general(
        pick, notes.astype(BF16), NT, preferred_element_type=F32
    ).astype(BF16)


def bundle_body(me, gate, down, value_weight, out):
    depth, width = gate.shape
    each = down.shape[0]
    out[:depth, :] = gate[...]
    wanted = value_weight[...]

    def split(value):
        high = value.astype(BF16).astype(F32)
        middle = (value - high).astype(BF16).astype(F32)
        low = (value - high - middle).astype(BF16).astype(F32)
        row = iota((EXTRA, value.shape[1]), 0)
        rows = jnp.where(row == 0, high, jnp.where(row == 1, middle, jnp.where(row == 2, low, 0.0)))
        return rows.astype(BF16)

    three = lax.dot_general(split(wanted), down[...], NT, preferred_element_type=F32)
    head = split(jnp.sum(three, axis=0, keepdims=True))
    place = iota((each, width), 1) == iota((each, width), 0) + me[0] * each
    out[depth:, :] = jnp.dot(head, place.astype(BF16), preferred_element_type=F32).astype(BF16)


def ring_owners(me, count):
    owners = [me]
    for step in range(1, count // 2):
        owners.append(lax.rem(me - step + count, count))
        owners.append(lax.rem(me + step, count))
    return owners + [lax.rem(me + count // 2, count)]


def join_body(high, low, out):
    rows = high.shape[0]
    out[:rows, :] = high[...]
    out[rows:, :] = low[...]


def forward_body(count, capacity, me, both, bundles, *rest):
    blocks, rest = rest[:count], rest[count:]
    above_out, gate_factor, up_factor, hidden_out, note_out, part_out, rows = rest
    slots, width = above_out.shape
    depth = width // count
    row = iota((slots, 2 * slots), 0)
    source = row + (row // capacity) * capacity
    column = iota((slots, 2 * slots), 1)
    rows[...] = jnp.dot(
        (column == source).astype(BF16), both[...], preferred_element_type=F32
    ).astype(BF16)
    above = jnp.dot(
        (column == source + capacity).astype(BF16), both[:, :width], preferred_element_type=F32
    )
    above_out[...] = above.astype(BF16)
    up_act = None
    for owner, ref in zip(ring_owners(me[0], count), blocks, strict=True):
        columns = pl.ds(pl.multiple_of(owner * depth, 128), depth)
        part = jnp.dot(rows[:, columns], ref[...], preferred_element_type=F32)
        up_act = part if up_act is None else up_act + part
    gate_act = None
    for owner in range(count):
        part = jnp.dot(
            rows[:, owner * depth : (owner + 1) * depth],
            bundles[owner, :depth, :],
            preferred_element_type=F32,
        )
        gate_act = part if gate_act is None else gate_act + part
    sig = jax.nn.sigmoid(gate_act)
    silu = gate_act * sig
    hidden = (silu * up_act).astype(BF16)
    hidden_out[...] = hidden
    gate_factor[...] = (up_act * (sig * (1.0 + gate_act * (1.0 - sig)))).astype(BF16)
    up_factor[...] = silu.astype(BF16)
    head = jnp.sum(
        jnp.sum(bundles[:, depth:, :].astype(F32), axis=0), axis=0, keepdims=True
    )
    proj = jnp.sum(hidden.astype(F32) * head, axis=1, keepdims=True)
    notes = rows[:, width:].astype(F32)
    gate = notes[:, 0:1] + notes[:, 1:2] + notes[:, 2:3]
    node = notes[:, 3:4]
    lane = iota((slots, LANES), 1)
    note_out[...] = jnp.where(lane == 0, gate, jnp.where(lane == 1, node, 0.0))
    share = gate * proj / jnp.maximum(notes[:, 4:5], 1.0)
    groups = slots // capacity
    by_node = jnp.where(iota((slots, 16), 1).astype(F32) == node, share, 0.0)
    gather = (iota((groups, slots), 1) // capacity == iota((groups, slots), 0)).astype(F32)
    part_out[...] = jnp.dot(
        gather, by_node, preferred_element_type=F32, precision=lax.Precision.HIGHEST
    )


def partial_body(capacity, sums, notes, above, value_weight, hidden, grad_out, partial_out, error_out):
    slots, width = above.shape
    errors = jnp.sum(sums[...], axis=0, keepdims=True)
    error_out[...] = errors
    lanes = errors.shape[1]
    gate, node = notes[:, 0:1], notes[:, 1:2].astype(I32)
    wanted = (iota((slots, 1), 0) // capacity) * 16 + node
    error = jnp.sum(
        jnp.where(iota((slots, lanes), 1) == wanted, errors, 0.0), axis=1, keepdims=True
    )
    grad = (above[...].astype(F32) + error * value_weight[...]).astype(BF16)
    out_grad = (gate * grad.astype(F32)).astype(BF16)
    grad_out[...] = out_grad
    partial_out[...] = lax.dot_general(
        hidden[...], out_grad, TN, preferred_element_type=F32
    ).astype(BF16)


def backward_body(count, me, grad, down, gate_factor, up_factor, hidden, bundles, *rest):
    blocks, (out, gate_back, up_back) = rest[:count], rest[count:]
    slots, width = grad.shape
    depth = width // count
    hidden_grad = lax.dot_general(grad[...], down[...], NT, preferred_element_type=F32)
    gate_back[...] = (hidden_grad * gate_factor[...].astype(F32)).astype(BF16)
    up_back[...] = (hidden_grad * up_factor[...].astype(F32)).astype(BF16)
    scaled = jnp.sum(hidden[...].astype(F32) * hidden_grad, axis=1, keepdims=True)
    high = scaled.astype(BF16).astype(F32)
    lane = iota((slots, LANES), 1)
    out[:, width:] = jnp.where(
        lane == 0, high, jnp.where(lane == 1, scaled - high, 0.0)
    ).astype(BF16)
    for owner, ref in zip(ring_owners(me[0], count), blocks, strict=True):
        part = lax.dot_general(up_back[...], ref[...], NT, preferred_element_type=F32)
        part = part + lax.dot_general(
            gate_back[...], bundles[owner, :depth, :], NT, preferred_element_type=F32
        )
        out[:, pl.ds(pl.multiple_of(owner * depth, 128), depth)] = part.astype(BF16)


def finish_body(returned, slot, above, value_weight, error, gates, sums, token_out, gate_out, down_out):
    slots = returned.shape[0]
    rows, width = above.shape
    pick = (iota((slots, rows), 0) == slot[...]).astype(BF16)
    mine = lax.dot_general(pick, returned[:, :width], TN, preferred_element_type=F32)
    grad = (above[...].astype(F32) + error[...] * value_weight[...]).astype(BF16)
    token_out[...] = (grad.astype(F32) + mine).astype(BF16)
    tail = lax.dot_general(returned[:, width:], pick, TN, preferred_element_type=F32)
    gate_out[...] = (tail[0:1, :] + tail[1:2, :]) / gates[...]
    down_out[...] = sums[...].astype(F32)


def local(
    tokens,
    gate_weight,
    up_weight,
    down_weight,
    value_weight,
    routes,
    gates,
    node_ids,
    lambda_targets,
    above_grad,
):
    experts = lax.axis_size("expert")
    replicas = lax.axis_size("replica")
    tok_rows, width = tokens.shape
    hidden_width = gate_weight.shape[2]
    capacity = 2 * tok_rows // experts
    slots = experts * capacity
    nodes = lambda_targets.shape[1]
    shape = jax.ShapeDtypeStruct
    value_row = value_weight[None, :]
    gate_row = gates.reshape(1, tok_rows)
    me = lax.axis_index("expert")
    my_replica = lax.axis_index("replica").astype(I32).reshape(1)

    bundle = call(
        bundle_body,
        shape((gate_weight.shape[1] + EXTRA, hidden_width), BF16),
        [SMEM, VMEM, VMEM, VMEM],
        0,
        4 * hidden_width * width // replicas,
    )(my_replica, gate_weight[0], down_weight[0], value_row)
    bundles = lax.all_gather(bundle, "replica", axis=0)

    block = up_weight[0]
    blocks = [block]
    right = left = block
    for step in range(1, replicas // 2):
        right, left = shift(right, 1), shift(left, -1)
        blocks += [right, left]
    half = block.shape[0] // 2
    blocks += [shift(right[:half], 1), shift(left[half:], -1)]

    blocks[-2:] = [
        call(join_body, shape(block.shape, BF16), [VMEM] * 2, JOIN_FLOPS, 4 * half * hidden_width)(
            *blocks[-2:]
        )
    ]

    both, slot_row = call(
        functools.partial(pack_body, experts, capacity),
        [shape((2 * slots, width + LANES), BF16), shape((1, tok_rows), I32)],
        [VMEM] * 5,
        4 * slots * tok_rows * width,
        8 * slots * width,
    )(routes.reshape(1, tok_rows), gate_row, node_ids, tokens, above_grad)
    both = exchange(both.reshape(experts, 2 * capacity, width + LANES))
    both = both.reshape(2 * slots, width + LANES)

    above_in, gate_factor, up_factor, hidden, notes, node_part, _ = call(
        functools.partial(forward_body, replicas, capacity),
        [
            shape((slots, width), BF16),
            shape((slots, hidden_width), BF16),
            shape((slots, hidden_width), BF16),
            shape((slots, hidden_width), BF16),
            shape((slots, LANES), F32),
            shape((experts, nodes), F32),
            shape((slots, width + LANES), BF16),
        ],
        [SMEM] + [VMEM] * (2 + replicas),
        4 * slots * hidden_width * width,
        4 * hidden_width * width,
    )(my_replica, both, bundles, *blocks)
    down = lax.all_gather(down_weight[0], "replica", axis=0, tiled=True)

    in_node = node_ids[0][:, None] == jnp.arange(nodes, dtype=I32)[None, :]
    in_node = in_node.astype(F32)
    token_value = jnp.sum(tokens.astype(F32) * value_row, axis=1)
    own = jnp.sum(in_node * token_value[:, None], axis=0) / jnp.sum(in_node, axis=0)
    own = own - lambda_targets[0]
    is_me = jnp.arange(experts, dtype=I32)[:, None] == me
    node_part = node_part + jnp.where(is_me, own[None, :], 0.0)
    sums = exchange(
        jnp.broadcast_to(node_part.reshape(1, experts * nodes), (experts, experts * nodes))
    )

    out_grad, partial, errors = call(
        functools.partial(partial_body, capacity),
        [
            shape((slots, width), BF16),
            shape((hidden_width, width), BF16),
            shape((1, experts * nodes), F32),
        ],
        [VMEM] * 5,
        2 * slots * hidden_width * width,
        4 * hidden_width * width,
    )(sums, notes, above_in, value_row, hidden)
    down_grad = lax.psum_scatter(partial, "replica", scatter_dimension=0, tiled=True)

    returned, _, _ = call(
        functools.partial(backward_body, replicas),
        [
            shape((slots, width + LANES), BF16),
            shape((slots, hidden_width), BF16),
            shape((slots, hidden_width), BF16),
        ],
        [SMEM] + [VMEM] * (6 + replicas),
        6 * slots * hidden_width * width,
        6 * hidden_width * width,
    )(my_replica, out_grad, down, gate_factor, up_factor, hidden, bundles, *blocks)
    returned = exchange(returned.reshape(experts, capacity, width + LANES))
    returned = returned.reshape(slots, width + LANES)

    node_error = jnp.sum(jnp.where(is_me, errors.reshape(experts, nodes), 0.0), axis=0)
    node_mean = node_error + lambda_targets[0]
    token_error = jnp.sum(in_node * node_error[None, :], axis=1)
    token_grad, gate_grad, down_out = call(
        finish_body,
        [
            shape(tokens.shape, BF16),
            shape(gate_row.shape, F32),
            shape(down_grad.shape, F32),
        ],
        [VMEM] * 7,
        2 * slots * tok_rows * width,
        8 * slots * width,
    )(returned, slot_row, above_grad, value_row, token_error[:, None], gate_row, down_grad)
    return token_grad, gate_grad.reshape(gates.shape), down_out[None], node_mean[None, :]


def solution(mesh):
    rows = P(("expert", "replica"), None)
    weight = P("expert", "replica", None)
    return jax.shard_map(
        local,
        mesh=mesh,
        in_specs=(rows, weight, weight, weight, P(), rows, rows, rows, rows, rows),
        out_specs=(rows, rows, weight, rows),
        check_vma=False,
    )
```
